32 devices in a mesh: gx: 8 (over z, x), gz: 4 (over y, core).
Axes of the slice: x: 2, y: 2, z: 4, core: 2. Of those that a mesh axis runs over, the one named last changes fastest.
Arguments:
- fields: float32 [3, 4096, 12288], P(None, 'gx', 'gz'), may hold values from -6 to 6
- register: float32 [3, 4096, 12288], P(None, 'gx', 'gz'), may hold values from -3 to 3
- source: float32 [4096, 12288], P('gx', 'gz'), may hold values from -0.25 to 0.25
- metric: float32 [4096], P('gx'), may hold values from 0.5 to 2
- curvature: float32 [4096], P('gx'), may hold values from -12 to 12
Outputs:
- new_fields: float32 [3, 4096, 12288], P(None, 'gx', 'gz')
- new_register: float32 [3, 4096, 12288], P(None, 'gx', 'gz')
- velocity: float32 [4096, 12288], P('gx', 'gz')
The draws below stay inside these ranges and needn't reach their ends.
All inputs are finite; a program needn't handle non-finite values. Where the reference program divides by a largest or mean magnitude, that divisor is 1e-20 or more.
Results may differ from the reference program's by a relative error of at most 0.0001.
Values sent between devices are 32-bit elements; how exact they have to be, the bound alone decides.
A program may use at most 320 MiB of HBM per device.

```python
import jax
import jax.numpy as jnp
from jax import lax

NX = 4096
NL = 12288


def shard_levels(own_key, extent, pieces, smallest, largest):
    factor_of, own = 1.0, jax.random.fold_in(own_key, 6)
    for dim, parts in pieces:
        draws = jnp.exp(jax.random.uniform(jax.random.fold_in(own, dim), (parts,), jnp.float32, smallest / len(pieces), largest / len(pieces)))
        factor_of = factor_of * jnp.repeat(draws, extent[dim] // parts).reshape([-1 if axis == dim else 1 for axis in range(len(extent))])
    return factor_of


def gaussian(stream_key, extent, deviation, limit, shards=(), held_as=jnp.bfloat16):
    drawn = jax.random.normal(stream_key, extent, jnp.float32) * deviation
    if len(shards) > 0:
        drawn = shard_levels(stream_key, extent, shards, -0.22, 0.18) * drawn
    return jnp.clip(drawn, min=-limit, max=limit).astype(held_as)


def setup_inputs(seed: int = 0) -> dict:
    streams_of = jax.random.split(jax.random.key(seed), 6)
    fields = gaussian(streams_of[0], (3, NX, NL), 1.0, 6.0, ((1, 8), (2, 4)), jnp.float32)
    register = gaussian(streams_of[1], (3, NX, NL), 0.5, 3.0, ((1, 8), (2, 4)), jnp.float32)
    source = gaussian(streams_of[2], (NX, NL), 0.03125, 0.25, ((0, 8), (1, 4)), jnp.float32)
    metric = jnp.clip(0.5 + 1.5 * jax.random.uniform(streams_of[3], (NX,), jnp.float32) ** shard_levels(streams_of[3], (NX,), ((0, 8),), -0.2, 0.2), 0.5, 2.0)
    curvature = gaussian(streams_of[4], (NX,), 3.0, 12.0, ((0, 8),), jnp.float32)
    return {"fields": fields, "register": register, "source": source, "metric": metric, "curvature": curvature}


ALPHA_ONE = 1.0 / 3.0
COEF_ONE = 14.0 / 9.0
WIDE_ONE = 1.0 / 9.0
ALPHA_TWO = 2.0 / 11.0
COEF_TWO = 12.0 / 11.0
WIDE_TWO = 3.0 / 11.0
VISCOSITY = 0.25
DIFFUSIVITY = 0.2
COURANT = 1.2
KEEP_FACTOR = -5.0 / 9.0
STEP_FACTOR = 15.0 / 16.0

def pad_cells(values):
    return jnp.pad(values, ((2, 2), (0, 0)))

def first_right(padded):
    return COEF_ONE / 2.0 * (padded[3:-1] - padded[1:-3]) + WIDE_ONE / 4.0 * (padded[4:] - padded[:-4])

def second_right(padded):
    centre = padded[2:-2]
    near = padded[3:-1] - 2.0 * centre + padded[1:-3]
    far = padded[4:] - 2.0 * centre + padded[:-4]
    return COEF_TWO * near + WIDE_TWO / 4.0 * far

def solve_lines(alpha, right_side):
    length = right_side.shape[0]
    offdiag = jnp.full((length,), alpha, jnp.float32)
    below_diag = offdiag.at[0].set(0.0)
    above_diag = offdiag.at[length - 1].set(0.0)
    diagonal = jnp.ones((length,), jnp.float32)
    return lax.linalg.tridiagonal_solve(below_diag, diagonal, above_diag, right_side)

def reference(fields, register, source, metric, curvature):
    stretch = metric[:, None]
    curving = curvature[:, None]
    scaled_source = source / stretch
    velocity = -(jnp.cumsum(scaled_source, axis=0) - 0.5 * scaled_source)
    max_rate = jnp.max(jnp.abs(velocity) * stretch + 4.0 * VISCOSITY * stretch * stretch)
    time_step = COURANT / max_rate
    velocity_x = stretch * solve_lines(ALPHA_ONE, first_right(pad_cells(velocity)))
    field_list = []
    register_list = []
    for component in range(3):
        field = fields[component]
        padded = pad_cells(field)
        slope = solve_lines(ALPHA_ONE, first_right(padded))
        bend = solve_lines(ALPHA_TWO, second_right(padded))
        field_x = stretch * slope
        field_xx = stretch * stretch * bend + curving * slope
        diffusion = VISCOSITY if component < 2 else DIFFUSIVITY
        tendency = -(velocity * field_x + field * velocity_x) + diffusion * field_xx
        updated = KEEP_FACTOR * register[component] + time_step * tendency
        register_list.append(updated)
        field_list.append(field + STEP_FACTOR * updated)
    return (jnp.stack(field_list), jnp.stack(register_list), velocity)
```

```python
import functools
import math

import jax
import jax.numpy as jnp
import numpy as np
from jax import lax
from jax.experimental import pallas as pl
from jax.experimental.pallas import tpu as pltpu
from jax.sharding import PartitionSpec as P

ALPHA_ONE = 1.0 / 3.0
COEF_ONE = 14.0 / 9.0
WIDE_ONE = 1.0 / 9.0
ALPHA_TWO = 2.0 / 11.0
COEF_TWO = 12.0 / 11.0
WIDE_TWO = 3.0 / 11.0
VISCOSITY = 0.25
DIFFUSIVITY = 0.2
DIFFUSIONS = (VISCOSITY, VISCOSITY, DIFFUSIVITY)
COURANT = 1.2
KEEP_FACTOR = -5.0 / 9.0
STEP_FACTOR = 15.0 / 16.0

MESH = pl.DeviceIdType.MESH
LANES = 128
LOADS = 4
SYSTEMS = 7

NEAR_ONE, FAR_ONE = COEF_ONE / 2.0, WIDE_ONE / 4.0
NEAR_TWO, FAR_TWO = COEF_TWO, WIDE_TWO / 4.0
STENCIL_ONE = (-FAR_ONE, -NEAR_ONE, 0.0, NEAR_ONE, FAR_ONE)
STENCIL_TWO = (FAR_TWO, NEAR_TWO, -2.0 * (NEAR_TWO + FAR_TWO), NEAR_TWO, FAR_TWO)
STENCIL_SUM = (
    -0.5 * FAR_ONE,
    -(0.5 * NEAR_ONE + FAR_ONE),
    -(NEAR_ONE + FAR_ONE),
    -(0.5 * NEAR_ONE + FAR_ONE),
    -0.5 * FAR_ONE,
)


def log_sinh(values):
    return values + np.log(1.0 - np.exp(-2.0 * values)) - math.log(2.0)


def inverse_table(alpha, length):
    ratio = 0.5 / alpha
    angle_value = math.log(ratio + math.sqrt(ratio * ratio - 1.0))
    row_index = np.arange(1, length + 1) * 1.0
    smaller = np.minimum(row_index[:, None], row_index[None, :])
    larger = np.maximum(row_index[:, None], row_index[None, :])
    magnitude = (
        np.exp(
            log_sinh(smaller * angle_value)
            + log_sinh((length + 1 - larger) * angle_value)
            - log_sinh(angle_value)
            - log_sinh((length + 1) * angle_value)
        )
        / alpha
    )
    sign_table = np.where((row_index[:, None] + row_index[None, :]) % 2 == 0, 1.0, -1.0)
    return magnitude * sign_table


def stencil_table(stencil, length):
    return sum(stencil[k + 2] * np.eye(length, k=k) for k in range(-2, 3))


def wide(table):
    return np.repeat(np.asarray(table, np.float32)[..., None], LANES, axis=-1)


def reach_of(column):
    kept = int(np.max(np.nonzero(np.asarray(column, np.float32))[0])) + 1
    return min(len(column), -(-kept // 16) * 16)


@functools.lru_cache(maxsize=None)
def tables(block):
    inv_one, inv_two = inverse_table(ALPHA_ONE, block), inverse_table(ALPHA_TWO, block)
    maps = (
        inv_one @ stencil_table(STENCIL_SUM, block),
        inv_one @ stencil_table(STENCIL_ONE, block),
        inv_two @ stencil_table(STENCIL_TWO, block),
    )
    reach = (reach_of(inv_one[:, 0]), reach_of(inv_two[:, 0]))
    columns = np.stack([inv_one[:, 0], inv_one[:, -1], inv_two[:, 0], inv_two[:, -1]])
    edge = max(reach_of(maps[k][0]) for k in range(3))
    firsts = np.stack([maps[k][0, :edge] for k in range(3)])
    lasts = np.stack([maps[k][-1, block - edge :] for k in range(3)])
    alphas = [ALPHA_ONE] * 4 + [ALPHA_TWO] * 3
    stencils = [STENCIL_SUM] + [STENCIL_ONE] * 3 + [STENCIL_TWO] * 3
    taus = [inv_one[0, 0]] * 4 + [inv_two[0, 0]] * 3
    joins = np.zeros((9, 8))
    for s in range(SYSTEMS):
        kappa = taus[s] * alphas[s]
        joins[:, s] = (
            stencils[s][3], stencils[s][4], stencils[s][1], stencils[s][0],
            1.0 / alphas[s], alphas[s], taus[s], kappa, 1.0 / (1.0 - kappa * kappa),
        )
    return dict(
        maps=np.stack(maps).astype(np.float32),
        reach=reach, columns=wide(columns), edge=edge, firsts=wide(firsts), lasts=wide(lasts),
        joins=wide(joins),
    )


def two_parts(values):
    high = values.astype(jnp.bfloat16)
    low = (values - high.astype(jnp.float32)).astype(jnp.bfloat16)
    return high, low


def lower_mask(block):
    rows = lax.broadcasted_iota(jnp.int32, (block, block), 0)
    columns = lax.broadcasted_iota(jnp.int32, (block, block), 1)
    return jnp.where(columns <= rows, 1.0, 0.0).astype(jnp.bfloat16)


def fill_column(column_ref, row_ref, change=lambda values: values):
    cells = row_ref.shape[1]
    size = min(LANES, cells)
    for r in range(0, cells, size):
        square = jnp.broadcast_to(row_ref[0:1, r : r + size], (LANES, size))
        column_ref[r : r + size] = change(jnp.transpose(square))


def spread(table, lanes):
    return jnp.concatenate([table] * (lanes // LANES), axis=-1) if lanes > LANES else table


def talk_kernel(
    group, bundles, block, edge, chunk,
    fields_ref, source_ref, metric_row_ref, firsts_ref, lasts_ref,
    halo_ref, offset_ref, step_ref,
    metric_ref, inverse_ref, mask_ref, src, run, tops, ends, totals, total_in, edges, halo, rate, rate_in, rate_two, rate_two_in,
    load_sem, tot_send, tot_recv, edge_send, edge_recv, one_send, one_recv, two_send, two_recv,
):
    cells, lines = src.shape
    parts = cells // block
    here, bundle = lax.axis_index("gx"), lax.axis_index("gz")
    pieces = lines // chunk
    broad = 512 if lines % 512 == 0 else chunk

    share = cells // LOADS
    loads = []
    for k in range(LOADS):
        rows = pl.ds(k * share, share)
        loads.append(pltpu.make_async_copy(source_ref.at[rows], src.at[rows], load_sem.at[k]))
    top_load = pltpu.make_async_copy(fields_ref.at[:, pl.ds(0, edge)], tops, load_sem.at[LOADS])
    end_load = pltpu.make_async_copy(fields_ref.at[:, pl.ds(cells - edge, edge)], ends, load_sem.at[LOADS + 1])
    for load in loads + [top_load, end_load]:
        load.start()

    barrier = pltpu.get_barrier_semaphore()

    def along(d):
        return (lax.rem(here + d, group), bundle)

    def across(d):
        return (here, lax.rem(bundle + d, bundles))

    @pl.loop(1, group)
    def _(d):
        pl.semaphore_signal(barrier, inc=1, device_id=along(d), device_id_type=MESH)

    @pl.loop(1, bundles)
    def _(d):
        pl.semaphore_signal(barrier, inc=1, device_id=across(d), device_id_type=MESH)

    fill_column(metric_ref, metric_row_ref)
    fill_column(inverse_ref, metric_row_ref, lambda values: 1.0 / values)
    mask = lower_mask(block)
    mask_ref[:, :block] = mask
    mask_ref[:, block:] = mask

    for k in range(LOADS):
        loads[k].wait()

        @pl.loop(0, lines // broad)
        def _(j):
            at = pl.ds(pl.multiple_of(j * broad, broad), broad)
            acc = jnp.zeros((8, broad), jnp.float32)
            for r in range(k * share, (k + 1) * share, 8):
                scaled = src[r : r + 8, at] * spread(inverse_ref[r : r + 8], broad)
                src[r : r + 8, at] = scaled
                acc = acc + scaled
            total = jnp.sum(acc, axis=0, keepdims=True)
            totals[0:1, at] = total if k == 0 else totals[0:1, at] + total

    pl.semaphore_wait(barrier, group + bundles - 2)

    def total_copy(d):
        return pltpu.make_async_remote_copy(
            src_ref=totals, dst_ref=total_in.at[d], send_sem=tot_send.at[d], recv_sem=tot_recv.at[d],
            device_id=along(d), device_id_type=MESH,
        )

    @pl.loop(1, group)
    def _(d):
        total_copy(d).start()

    top_load.wait()
    end_load.wait()

    edges[0, 7:8, :] = jnp.zeros((1, lines), jnp.float32)
    edges[1, 7:8, :] = jnp.zeros((1, lines), jnp.float32)

    @pl.loop(0, pieces)
    def _(j):
        at = pl.ds(pl.multiple_of(j * chunk, chunk), chunk)
        for side, weights in ((0, lasts_ref), (1, firsts_ref)):
            base = cells - edge if side == 0 else 0
            acc = jnp.zeros((8, chunk), jnp.float32)
            for r in range(0, edge, 8):
                acc = acc + src[base + r : base + r + 8, at] * spread(weights[0, r : r + 8], chunk)
            edges[side, 0:1, at] = jnp.sum(acc, axis=0, keepdims=True)
            outer = cells - 1 if side == 0 else 0
            inner = cells - 2 if side == 0 else 1
            edges[side, 8:9, at] = src[outer : outer + 1, at]
            edges[side, 12:13, at] = src[inner : inner + 1, at]
            rows = ends if side == 0 else tops
            for c in range(3):
                one = jnp.zeros((8, chunk), jnp.float32)
                two = jnp.zeros((8, chunk), jnp.float32)
                for r in range(0, edge, 8):
                    value = rows[c, r : r + 8, at]
                    one = one + value * spread(weights[1, r : r + 8], chunk)
                    two = two + value * spread(weights[2, r : r + 8], chunk)
                edges[side, 1 + c : 2 + c, at] = jnp.sum(one, axis=0, keepdims=True)
                edges[side, 4 + c : 5 + c, at] = jnp.sum(two, axis=0, keepdims=True)
                outer = edge - 1 if side == 0 else 0
                inner = edge - 2 if side == 0 else 1
                edges[side, 9 + c : 10 + c, at] = rows[c, outer : outer + 1, at]
                edges[side, 13 + c : 14 + c, at] = rows[c, inner : inner + 1, at]

    edge_copies = [
        pltpu.make_async_remote_copy(
            src_ref=edges.at[side], dst_ref=halo.at[side], send_sem=edge_send.at[side],
            recv_sem=edge_recv.at[side], device_id=along(1 if side == 0 else group - 1), device_id_type=MESH,
        )
        for side in range(2)
    ]
    for copy in edge_copies:
        copy.start()

    @pl.loop(0, pieces)
    def _(j):
        at = pl.ds(pl.multiple_of(j * chunk, chunk), chunk)
        before = jnp.zeros((1, chunk), jnp.float32)
        for k in range(parts):
            scaled = src[k * block : (k + 1) * block, at]
            high, low = two_parts(scaled)
            sums = jnp.dot(mask_ref[...], jnp.concatenate([high, low], axis=0), preferred_element_type=jnp.float32)
            run[k * block : (k + 1) * block, at] = before + sums - 0.5 * scaled
            before = before + sums[block - 1 : block]

    @pl.loop(1, group)
    def _(d):
        total_copy(d).wait()

    def earlier(d, acc):
        return acc + jnp.where(d <= here, total_in[d], 0.0)

    offset = lax.fori_loop(1, group, earlier, jnp.zeros((1, lines), jnp.float32))
    offset_ref[0:1, :] = offset
    offset_ref[1:8, :] = jnp.zeros((7, lines), jnp.float32)

    rate[...] = jnp.zeros((8, LANES), jnp.float32)

    @pl.loop(0, lines // broad)
    def _(j):
        at = pl.ds(pl.multiple_of(j * broad, broad), broad)
        before = offset_ref[0:1, at]
        acc = jnp.zeros((8, broad), jnp.float32)
        for r in range(0, cells, 8):
            stretch = spread(metric_ref[r : r + 8], broad)
            speed = jnp.abs(before + run[r : r + 8, at])
            acc = jnp.maximum(acc, speed * stretch + 4.0 * VISCOSITY * stretch * stretch)
        for k in range(broad // LANES):
            rate[...] = jnp.maximum(rate[...], acc[:, k * LANES : (k + 1) * LANES])

    def one_copy(d):
        return pltpu.make_async_remote_copy(
            src_ref=rate, dst_ref=rate_in.at[d], send_sem=one_send.at[d], recv_sem=one_recv.at[d],
            device_id=along(d), device_id_type=MESH,
        )

    def two_copy(d):
        return pltpu.make_async_remote_copy(
            src_ref=rate_two, dst_ref=rate_two_in.at[d], send_sem=two_send.at[d], recv_sem=two_recv.at[d],
            device_id=across(d), device_id_type=MESH,
        )

    @pl.loop(1, group)
    def _(d):
        one_copy(d).start()

    @pl.loop(1, group)
    def _(d):
        one_copy(d).wait()

    rate_two[...] = lax.fori_loop(1, group, lambda d, acc: jnp.maximum(acc, rate_in[d]), rate[...])

    @pl.loop(1, bundles)
    def _(d):
        two_copy(d).start()

    @pl.loop(1, bundles)
    def _(d):
        two_copy(d).wait()

    largest = lax.fori_loop(1, bundles, lambda d, acc: jnp.maximum(acc, rate_two_in[d]), rate_two[...])
    place = jnp.full((1, LANES), here, jnp.int32)
    step_ref[...] = COURANT / jnp.broadcast_to(jnp.max(largest), (8, LANES))
    step_ref[1:2, :] = jnp.where(place > 0, 1.0, 0.0)
    step_ref[2:3, :] = jnp.where(place < group - 1, 1.0, 0.0)

    for copy in edge_copies:
        copy.wait()
    halo_ref[...] = halo[...]


def talk(fields, source, metric, const, group, bundles, block):
    cells, lines = source.shape
    chunk = 256 if lines % 256 == 0 else LANES
    edge = const["edge"]
    parts = cells // block
    vmem, dma = pltpu.VMEM, pltpu.SemaphoreType.DMA
    f32 = jnp.float32
    whole = pl.BlockSpec(memory_space=pltpu.VMEM)
    held = pl.BlockSpec(memory_space=pl.ANY)
    return pl.pallas_call(
        functools.partial(talk_kernel, group, bundles, block, edge, chunk),
        out_shape=(
            jax.ShapeDtypeStruct((2, 16, lines), f32),
            jax.ShapeDtypeStruct((8, lines), f32),
            jax.ShapeDtypeStruct((8, LANES), f32),
        ),
        in_specs=[held, held] + [whole] * 3,
        out_specs=(whole,) * 3,
        scratch_shapes=[
            vmem((cells, LANES), f32), vmem((cells, LANES), f32), vmem((block, 2 * block), jnp.bfloat16),
            vmem((cells, lines), f32), vmem((cells, lines), f32),
            vmem((3, edge, lines), f32), vmem((3, edge, lines), f32),
            vmem((1, lines), f32), vmem((group, 1, lines), f32),
            vmem((2, 16, lines), f32), vmem((2, 16, lines), f32),
            vmem((8, LANES), f32), vmem((group, 8, LANES), f32),
            vmem((8, LANES), f32), vmem((bundles, 8, LANES), f32),
            dma((LOADS + 2,)), dma((group,)), dma((group,)), dma((2,)), dma((2,)),
            dma((group,)), dma((group,)), dma((bundles,)), dma((bundles,)),
        ],
        compiler_params=pltpu.CompilerParams(
            collective_id=0, has_side_effects=True, vmem_limit_bytes=48 * 2**20
        ),
        name="talk",
    )(
        fields, source, metric, jnp.asarray(const["firsts"]), jnp.asarray(const["lasts"]),
    )


def join(coef, last, outer_l, inner_l, first, outer_r, inner_r):
    rp1, rp2, rm1, rm2, over, alpha, tau, kappa, scale = coef
    edge_l = rp2 * outer_r * over
    edge_r = rm2 * outer_l * over
    near_l = rp1 * outer_r + rp2 * inner_r - edge_l
    near_r = rm1 * outer_l + rm2 * inner_l - edge_r
    a = last + tau * near_l + edge_l
    b = first + tau * near_r + edge_r
    first_x = (b - kappa * a) * scale
    last_x = (a - kappa * b) * scale
    return near_l - alpha * first_x, edge_l, near_r - alpha * last_x, edge_r


def main_kernel(
    block, reach, rows_at_once,
    step_ref, fields_ref, register_ref, source_ref, metric_row_ref, curving_row_ref,
    offset_ref, halo_ref, maps_ref, columns_ref, joins_ref,
    new_fields_ref, new_register_ref, velocity_ref,
    inverse_ref, metric_ref, curving_ref, source_map_ref, field_map_ref,
    solved, firsts, lasts, cells_at, add,
):
    cells, lines = source_ref.shape
    parts = cells // block
    f32 = jnp.float32

    @pl.when(pl.program_id(0) == 0)
    def _():
        fill_column(metric_ref, metric_row_ref)
        fill_column(inverse_ref, metric_row_ref, lambda values: 1.0 / values)
        fill_column(curving_ref, curving_row_ref)
        mask = lower_mask(block)
        source_map_ref[:block, :block] = mask
        source_map_ref[:block, block : 2 * block] = mask
        source_map_ref[:block, 2 * block :] = jnp.zeros((block, block), jnp.bfloat16)
        for m, (table, start) in enumerate(((source_map_ref, block), (field_map_ref, 0), (field_map_ref, block))):
            high, low = two_parts(maps_ref[m])
            table[start : start + block, :block] = high
            table[start : start + block, block : 2 * block] = high
            table[start : start + block, 2 * block :] = low

    for k in range(parts):
        rows = slice(k * block, (k + 1) * block)
        for c in range(4):
            if c == 0:
                value = source_ref[rows] * spread(inverse_ref[rows], lines)
                table = source_map_ref
            else:
                value = fields_ref[c - 1, rows]
                table = field_map_ref
            high, low = two_parts(value)
            solved[k, c] = jnp.dot(
                table[...], jnp.concatenate([high, low, high], axis=0), preferred_element_type=f32
            )
            for e, r in enumerate((0, 1, block - 1, block - 2)):
                row = value[r : r + 1]
                cells_at[k, e, c : c + 1] = row
                if c > 0:
                    cells_at[k, e, 3 + c : 4 + c] = row
        for into, r in ((firsts, 0), (lasts, block - 1)):
            into[k, 0:1] = solved[k, 0, block + r : block + r + 1]
            for c in range(3):
                into[k, 1 + c : 2 + c] = solved[k, 1 + c, r : r + 1]
                into[k, 4 + c : 5 + c] = solved[k, 1 + c, block + r : block + r + 1]
            into[k, 7:8] = jnp.zeros((1, lines), f32)
        for e in range(4):
            cells_at[k, e, 7:8] = jnp.zeros((1, lines), f32)

    coef = [spread(joins_ref[i], lines) for i in range(9)]
    before = [offset_ref[0:1, :]]
    for k in range(parts):
        before.append(before[-1] + solved[k, 0, block - 1 : block])

    def far_cells(side, start):
        own = halo_ref[side, start : start + 4]
        return jnp.concatenate([own, own[1:4], jnp.zeros((1, lines), f32)], axis=0)

    has_before, has_after = spread(step_ref[1:2], lines), spread(step_ref[2:3], lines)
    _, _, near, at_edge = join(
        coef, halo_ref[0, 0:8], far_cells(0, 8), far_cells(0, 12), firsts[0], cells_at[0, 0], cells_at[0, 1]
    )
    add[0, 0], add[0, 1] = near * has_before, at_edge * has_before
    for k in range(parts - 1):
        add[k, 2], add[k, 3], add[k + 1, 0], add[k + 1, 1] = join(
            coef, lasts[k], cells_at[k, 2], cells_at[k, 3],
            firsts[k + 1], cells_at[k + 1, 0], cells_at[k + 1, 1],
        )
    k = parts - 1
    near, at_edge, _, _ = join(
        coef, lasts[k], cells_at[k, 2], cells_at[k, 3], halo_ref[1, 0:8], far_cells(1, 8), far_cells(1, 12)
    )
    add[k, 2], add[k, 3] = near * has_after, at_edge * has_after
    beyond = before[parts] * (1.0 - has_after)
    add[k, 2, 0:1] = add[k, 2, 0:1] + (NEAR_ONE + FAR_ONE - FAR_ONE / ALPHA_ONE) * beyond
    add[k, 3, 0:1] = add[k, 3, 0:1] + (FAR_ONE / ALPHA_ONE) * beyond

    time_step = spread(step_ref[0:1], lines)
    for k in range(parts):
        places = [(0, block)] + [(1 + c, 0) for c in range(3)] + [(1 + c, block) for c in range(3)]
        for s, (slot, start) in enumerate(places):
            solved[k, slot, start : start + 1] += add[k, 1, s : s + 1]
            solved[k, slot, start + block - 1 : start + block] += add[k, 3, s : s + 1]

        for r in range(0, block, rows_at_once):
            rows = slice(k * block + r, k * block + r + rows_at_once)

            def whole(s):
                slot, start = places[s]
                kind = 0 if s < 4 else 1
                value = solved[k, slot, start + r : start + r + rows_at_once]
                if r < reach[kind]:
                    column = spread(columns_ref[2 * kind, r : r + rows_at_once], lines)
                    value = value + column * add[k, 0, s : s + 1]
                if r + rows_at_once > block - reach[kind]:
                    column = spread(columns_ref[2 * kind + 1, r : r + rows_at_once], lines)
                    value = value + column * add[k, 2, s : s + 1]
                return value

            stretch = spread(metric_ref[rows], lines)
            curving = spread(curving_ref[rows], lines)
            scaled = source_ref[rows] * spread(inverse_ref[rows], lines)
            velocity = 0.5 * scaled - (before[k] + solved[k, 0, r : r + rows_at_once])
            velocity_ref[rows] = velocity
            carried = velocity * stretch
            squeezed = (time_step * stretch) * whole(0)
            bent = time_step * stretch * stretch
            for c in range(3):
                on_slope = time_step * (DIFFUSIONS[c] * curving - carried)
                field = fields_ref[c, rows]
                change = on_slope * whole(1 + c) + (DIFFUSIONS[c] * bent) * whole(4 + c) - field * squeezed
                updated = KEEP_FACTOR * register_ref[c, rows] + change
                new_register_ref[c, rows] = updated
                new_fields_ref[c, rows] = field + STEP_FACTOR * updated


def compute(fields, register, source, metric, curving, halo, offset, step, const, block):
    cells, lines = source.shape
    width = 256 if lines % 256 == 0 else LANES
    parts = cells // block
    f32 = jnp.float32

    def fixed(array):
        rank = array.ndim
        return pl.BlockSpec(array.shape, lambda j: (0,) * rank)

    three = pl.BlockSpec((3, cells, width), lambda j: (0, 0, j))
    flat = pl.BlockSpec((cells, width), lambda j: (0, j))
    maps, columns, joins = jnp.asarray(const["maps"]), jnp.asarray(const["columns"]), jnp.asarray(const["joins"])
    return pl.pallas_call(
        functools.partial(main_kernel, block, const["reach"], min(32, block)),
        grid=(lines // width,),
        out_shape=(
            jax.ShapeDtypeStruct(fields.shape, f32),
            jax.ShapeDtypeStruct(register.shape, f32),
            jax.ShapeDtypeStruct(source.shape, f32),
        ),
        in_specs=[
            fixed(step), three, three, flat, fixed(metric), fixed(curving),
            pl.BlockSpec((8, width), lambda j: (0, j)),
            pl.BlockSpec((2, 16, width), lambda j: (0, 0, j)),
            fixed(maps), fixed(columns), fixed(joins),
        ],
        out_specs=(three, three, flat),
        scratch_shapes=[
            pltpu.VMEM((cells, LANES), f32), pltpu.VMEM((cells, LANES), f32), pltpu.VMEM((cells, LANES), f32),
            pltpu.VMEM((2 * block, 3 * block), jnp.bfloat16), pltpu.VMEM((2 * block, 3 * block), jnp.bfloat16),
            pltpu.VMEM((parts, 4, 2 * block, width), f32),
            pltpu.VMEM((parts, 8, width), f32),
            pltpu.VMEM((parts, 8, width), f32),
            pltpu.VMEM((parts, 4, 8, width), f32),
            pltpu.VMEM((parts, 4, 8, width), f32),
        ],
        compiler_params=pltpu.CompilerParams(vmem_limit_bytes=48 * 2**20),
        name="compute",
    )(
        step, fields, register, source, metric, curving, offset, halo, maps, columns, joins,
    )


def local(fields, register, source, metric, curvature):
    group, bundles = lax.axis_size("gx"), lax.axis_size("gz")
    cells = source.shape[0]
    block = min(256, cells)
    const = tables(block)
    metric_row, curving_row = metric.reshape(1, cells), curvature.reshape(1, cells)
    halo, offset, step = talk(fields, source, metric_row, const, group, bundles, block)
    return compute(fields, register, source, metric_row, curving_row, halo, offset, step, const, block)


def solution(mesh):
    placed = (P(None, "gx", "gz"), P(None, "gx", "gz"), P("gx", "gz"), P("gx"), P("gx"))
    return jax.shard_map(
        local,
        mesh=mesh,
        in_specs=placed,
        out_specs=(P(None, "gx", "gz"), P(None, "gx", "gz"), P("gx", "gz")),
        check_vma=False,
    )
```

```python
import functools
import math

import jax
import jax.numpy as jnp
import numpy as np
from jax import lax
from jax.experimental import pallas as pl
from jax.experimental.pallas import tpu as pltpu
from jax.sharding import PartitionSpec as P

ALPHA_ONE = 1.0 / 3.0
COEF_ONE = 14.0 / 9.0
WIDE_ONE = 1.0 / 9.0
ALPHA_TWO = 2.0 / 11.0
COEF_TWO = 12.0 / 11.0
WIDE_TWO = 3.0 / 11.0
VISCOSITY = 0.25
DIFFUSIVITY = 0.2
DIFFUSIONS = (VISCOSITY, VISCOSITY, DIFFUSIVITY)
COURANT = 1.2
KEEP_FACTOR = -5.0 / 9.0
STEP_FACTOR = 15.0 / 16.0

MESH = pl.DeviceIdType.MESH
LANES = 128
LOADS = 4
SYSTEMS = 7

NEAR_ONE, FAR_ONE = COEF_ONE / 2.0, WIDE_ONE / 4.0
NEAR_TWO, FAR_TWO = COEF_TWO, WIDE_TWO / 4.0
STENCIL_ONE = (-FAR_ONE, -NEAR_ONE, 0.0, NEAR_ONE, FAR_ONE)
STENCIL_TWO = (FAR_TWO, NEAR_TWO, -2.0 * (NEAR_TWO + FAR_TWO), NEAR_TWO, FAR_TWO)
STENCIL_SUM = (
    -0.5 * FAR_ONE,
    -(0.5 * NEAR_ONE + FAR_ONE),
    -(NEAR_ONE + FAR_ONE),
    -(0.5 * NEAR_ONE + FAR_ONE),
    -0.5 * FAR_ONE,
)


def log_sinh(values):
    return values + np.log(1.0 - np.exp(-2.0 * values)) - math.log(2.0)


def inverse_table(alpha, length):
    ratio = 0.5 / alpha
    angle_value = math.log(ratio + math.sqrt(ratio * ratio - 1.0))
    row_index = np.arange(1, length + 1) * 1.0
    smaller = np.minimum(row_index[:, None], row_index[None, :])
    larger = np.maximum(row_index[:, None], row_index[None, :])
    magnitude = (
        np.exp(
            log_sinh(smaller * angle_value)
            + log_sinh((length + 1 - larger) * angle_value)
            - log_sinh(angle_value)
            - log_sinh((length + 1) * angle_value)
        )
        / alpha
    )
    sign_table = np.where((row_index[:, None] + row_index[None, :]) % 2 == 0, 1.0, -1.0)
    return magnitude * sign_table


def stencil_table(stencil, length):
    return sum(stencil[k + 2] * np.eye(length, k=k) for k in range(-2, 3))


def wide(table):
    return np.repeat(np.asarray(table, np.float32)[..., None], LANES, axis=-1)


def reach_of(column):
    kept = int(np.max(np.nonzero(np.asarray(column, np.float32))[0])) + 1
    return min(len(column), -(-kept // 16) * 16)


@functools.lru_cache(maxsize=None)
def tables(block):
    inv_one, inv_two = inverse_table(ALPHA_ONE, block), inverse_table(ALPHA_TWO, block)
    maps = (
        inv_one @ stencil_table(STENCIL_SUM, block),
        inv_one @ stencil_table(STENCIL_ONE, block),
        inv_two @ stencil_table(STENCIL_TWO, block),
    )
    reach = (reach_of(inv_one[:, 0]), reach_of(inv_two[:, 0]))
    columns = np.stack([inv_one[:, 0], inv_one[:, -1], inv_two[:, 0], inv_two[:, -1]])
    edge = max(reach_of(maps[k][0]) for k in range(3))
    weights = np.zeros((8, LANES), np.float32)
    for k in range(3):
        weights[k, :edge] = maps[k][0, :edge]
        weights[3 + k, :edge] = maps[k][-1, block - edge :]
    alphas = [ALPHA_ONE] * 4 + [ALPHA_TWO] * 3
    stencils = [STENCIL_SUM] + [STENCIL_ONE] * 3 + [STENCIL_TWO] * 3
    taus = [inv_one[0, 0]] * 4 + [inv_two[0, 0]] * 3
    joins = np.zeros((9, 8))
    for s in range(SYSTEMS):
        kappa = taus[s] * alphas[s]
        joins[:, s] = (
            stencils[s][3], stencils[s][4], stencils[s][1], stencils[s][0],
            1.0 / alphas[s], alphas[s], taus[s], kappa, 1.0 / (1.0 - kappa * kappa),
        )
    return dict(
        maps=np.stack(maps).astype(np.float32),
        reach=reach, columns=wide(columns), edge=edge, weights=weights,
        joins=wide(joins),
    )


def two_parts(values):
    high = values.astype(jnp.bfloat16)
    low = (values - high.astype(jnp.float32)).astype(jnp.bfloat16)
    return high, low


def lower_mask(block):
    rows = lax.broadcasted_iota(jnp.int32, (block, block), 0)
    columns = lax.broadcasted_iota(jnp.int32, (block, block), 1)
    return jnp.where(columns <= rows, 1.0, 0.0).astype(jnp.bfloat16)


def fill_column(column_ref, row_ref, change=lambda values: values):
    cells = row_ref.shape[1]
    size = min(LANES, cells)
    for r in range(0, cells, size):
        square = jnp.broadcast_to(row_ref[0:1, r : r + size], (LANES, size))
        column_ref[r : r + size] = change(jnp.transpose(square))


def spread(table, lanes):
    return jnp.concatenate([table] * (lanes // LANES), axis=-1) if lanes > LANES else table


def talk_kernel(
    group, bundles, block, edge, chunk,
    fields_ref, source_ref, metric_in_ref, weights_in_ref,
    halo_ref, offset_ref, step_ref,
    metric_row_ref, weights_row_ref, weights_ref, metric_ref, inverse_ref, mask_ref, src, run, tops, ends, totals, total_in, edges, halo, rate, rate_in, rate_two, rate_two_in,
    load_sem, tot_send, tot_recv, edge_send, edge_recv, one_send, one_recv, two_send, two_recv,
):
    cells, lines = src.shape
    parts = cells // block
    here, bundle = lax.axis_index("gx"), lax.axis_index("gz")
    pieces = lines // chunk
    broad = 512 if lines % 512 == 0 else chunk

    share = cells // LOADS
    metric_load = pltpu.make_async_copy(metric_in_ref, metric_row_ref, load_sem.at[LOADS + 2])
    weights_load = pltpu.make_async_copy(weights_in_ref, weights_row_ref, load_sem.at[LOADS + 3])
    loads = []
    for k in range(LOADS):
        rows = pl.ds(k * share, share)
        loads.append(pltpu.make_async_copy(source_ref.at[rows], src.at[rows], load_sem.at[k]))
    top_load = pltpu.make_async_copy(fields_ref.at[:, pl.ds(0, edge)], tops, load_sem.at[LOADS])
    end_load = pltpu.make_async_copy(fields_ref.at[:, pl.ds(cells - edge, edge)], ends, load_sem.at[LOADS + 1])
    for load in [metric_load, weights_load] + loads:
        load.start()

    barrier = pltpu.get_barrier_semaphore()

    def along(d):
        return (lax.rem(here + d, group), bundle)

    def across(d):
        return (here, lax.rem(bundle + d, bundles))

    @pl.loop(1, group)
    def _(d):
        pl.semaphore_signal(barrier, inc=1, device_id=along(d), device_id_type=MESH)

    @pl.loop(1, bundles)
    def _(d):
        pl.semaphore_signal(barrier, inc=1, device_id=across(d), device_id_type=MESH)

    metric_load.wait()
    weights_load.wait()
    fill_column(metric_ref, metric_row_ref)
    fill_column(inverse_ref, metric_row_ref, lambda values: 1.0 / values)
    for m in range(6):
        weights_ref[m] = jnp.transpose(jnp.broadcast_to(weights_row_ref[m : m + 1], (LANES, LANES)))
    mask = lower_mask(block)
    mask_ref[:, :block] = mask
    mask_ref[:, block:] = mask

    for k in range(LOADS):
        loads[k].wait()
        if k == LOADS - 2:
            top_load.start()
            end_load.start()

        @pl.loop(0, lines // broad)
        def _(j):
            at = pl.ds(pl.multiple_of(j * broad, broad), broad)
            acc = jnp.zeros((8, broad), jnp.float32)
            for r in range(k * share, (k + 1) * share, 8):
                scaled = src[r : r + 8, at] * spread(inverse_ref[r : r + 8], broad)
                src[r : r + 8, at] = scaled
                acc = acc + scaled
            total = jnp.sum(acc, axis=0, keepdims=True)
            totals[0:1, at] = total if k == 0 else totals[0:1, at] + total

    pl.semaphore_wait(barrier, group + bundles - 2)

    def total_copy(d):
        return pltpu.make_async_remote_copy(
            src_ref=totals, dst_ref=total_in.at[d], send_sem=tot_send.at[d], recv_sem=tot_recv.at[d],
            device_id=along(d), device_id_type=MESH,
        )

    @pl.loop(1, group)
    def _(d):
        total_copy(d).start()

    top_load.wait()
    end_load.wait()

    edges[0, 7:8, :] = jnp.zeros((1, lines), jnp.float32)
    edges[1, 7:8, :] = jnp.zeros((1, lines), jnp.float32)

    @pl.loop(0, pieces)
    def _(j):
        at = pl.ds(pl.multiple_of(j * chunk, chunk), chunk)
        for side, first_weight in ((0, 3), (1, 0)):
            base = cells - edge if side == 0 else 0
            acc = jnp.zeros((8, chunk), jnp.float32)
            for r in range(0, edge, 8):
                acc = acc + src[base + r : base + r + 8, at] * spread(weights_ref[first_weight, r : r + 8], chunk)
            edges[side, 0:1, at] = jnp.sum(acc, axis=0, keepdims=True)
            outer = cells - 1 if side == 0 else 0
            inner = cells - 2 if side == 0 else 1
            edges[side, 8:9, at] = src[outer : outer + 1, at]
            edges[side, 12:13, at] = src[inner : inner + 1, at]
            rows = ends if side == 0 else tops
            for c in range(3):
                one = jnp.zeros((8, chunk), jnp.float32)
                two = jnp.zeros((8, chunk), jnp.float32)
                for r in range(0, edge, 8):
                    value = rows[c, r : r + 8, at]
                    one = one + value * spread(weights_ref[first_weight + 1, r : r + 8], chunk)
                    two = two + value * spread(weights_ref[first_weight + 2, r : r + 8], chunk)
                edges[side, 1 + c : 2 + c, at] = jnp.sum(one, axis=0, keepdims=True)
                edges[side, 4 + c : 5 + c, at] = jnp.sum(two, axis=0, keepdims=True)
                outer = edge - 1 if side == 0 else 0
                inner = edge - 2 if side == 0 else 1
                edges[side, 9 + c : 10 + c, at] = rows[c, outer : outer + 1, at]
                edges[side, 13 + c : 14 + c, at] = rows[c, inner : inner + 1, at]

    edge_copies = [
        pltpu.make_async_remote_copy(
            src_ref=edges.at[side], dst_ref=halo.at[side], send_sem=edge_send.at[side],
            recv_sem=edge_recv.at[side], device_id=along(1 if side == 0 else group - 1), device_id_type=MESH,
        )
        for side in range(2)
    ]
    @pl.when(here < group - 1)
    def _():
        edge_copies[0].start()

    @pl.when(here > 0)
    def _():
        edge_copies[1].start()

    @pl.loop(0, pieces)
    def _(j):
        at = pl.ds(pl.multiple_of(j * chunk, chunk), chunk)
        before = jnp.zeros((1, chunk), jnp.float32)
        for k in range(parts):
            scaled = src[k * block : (k + 1) * block, at]
            high, low = two_parts(scaled)
            sums = jnp.dot(mask_ref[...], jnp.concatenate([high, low], axis=0), preferred_element_type=jnp.float32)
            run[k * block : (k + 1) * block, at] = before + sums - 0.5 * scaled
            before = before + sums[block - 1 : block]

    @pl.loop(1, group)
    def _(d):
        total_copy(d).wait()

    def earlier(d, acc):
        return acc + jnp.where(d <= here, total_in[d], 0.0)

    offset = lax.fori_loop(1, group, earlier, jnp.zeros((1, lines), jnp.float32))
    offset_ref[0:1, :] = offset
    offset_ref[1:8, :] = jnp.zeros((7, lines), jnp.float32)

    rate[...] = jnp.zeros((8, LANES), jnp.float32)

    @pl.loop(0, lines // broad)
    def _(j):
        at = pl.ds(pl.multiple_of(j * broad, broad), broad)
        before = offset_ref[0:1, at]
        acc = jnp.zeros((8, broad), jnp.float32)
        for r in range(0, cells, 8):
            stretch = spread(metric_ref[r : r + 8], broad)
            speed = jnp.abs(before + run[r : r + 8, at])
            acc = jnp.maximum(acc, speed * stretch + 4.0 * VISCOSITY * stretch * stretch)
        for k in range(broad // LANES):
            rate[...] = jnp.maximum(rate[...], acc[:, k * LANES : (k + 1) * LANES])

    def one_copy(d):
        return pltpu.make_async_remote_copy(
            src_ref=rate, dst_ref=rate_in.at[d], send_sem=one_send.at[d], recv_sem=one_recv.at[d],
            device_id=along(d), device_id_type=MESH,
        )

    def two_copy(d):
        return pltpu.make_async_remote_copy(
            src_ref=rate_two, dst_ref=rate_two_in.at[d], send_sem=two_send.at[d], recv_sem=two_recv.at[d],
            device_id=across(d), device_id_type=MESH,
        )

    @pl.loop(1, group)
    def _(d):
        one_copy(d).start()

    @pl.loop(1, group)
    def _(d):
        one_copy(d).wait()

    rate_two[...] = lax.fori_loop(1, group, lambda d, acc: jnp.maximum(acc, rate_in[d]), rate[...])

    @pl.loop(1, bundles)
    def _(d):
        two_copy(d).start()

    @pl.loop(1, bundles)
    def _(d):
        two_copy(d).wait()

    largest = lax.fori_loop(1, bundles, lambda d, acc: jnp.maximum(acc, rate_two_in[d]), rate_two[...])
    place = jnp.full((1, LANES), here, jnp.int32)
    step_ref[...] = COURANT / jnp.broadcast_to(jnp.max(largest), (8, LANES))
    step_ref[1:2, :] = jnp.where(place > 0, 1.0, 0.0)
    step_ref[2:3, :] = jnp.where(place < group - 1, 1.0, 0.0)

    halo_ref[...] = jnp.zeros((2, 16, lines), jnp.float32)

    @pl.when(here < group - 1)
    def _():
        edge_copies[0].wait_send()
        edge_copies[1].wait_recv()
        halo_ref[1] = halo[1]

    @pl.when(here > 0)
    def _():
        edge_copies[1].wait_send()
        edge_copies[0].wait_recv()
        halo_ref[0] = halo[0]


def talk(fields, source, metric, const, group, bundles, block):
    cells, lines = source.shape
    chunk = 256 if lines % 256 == 0 else LANES
    edge = const["edge"]
    parts = cells // block
    vmem, dma = pltpu.VMEM, pltpu.SemaphoreType.DMA
    f32 = jnp.float32
    whole = pl.BlockSpec(memory_space=pltpu.VMEM)
    held = pl.BlockSpec(memory_space=pl.ANY)
    return pl.pallas_call(
        functools.partial(talk_kernel, group, bundles, block, edge, chunk),
        out_shape=(
            jax.ShapeDtypeStruct((2, 16, lines), f32),
            jax.ShapeDtypeStruct((8, lines), f32),
            jax.ShapeDtypeStruct((8, LANES), f32),
        ),
        in_specs=[held] * 4,
        out_specs=(whole,) * 3,
        scratch_shapes=[
            vmem((1, cells), f32), vmem((8, LANES), f32), vmem((6, LANES, LANES), f32),
            vmem((cells, LANES), f32), vmem((cells, LANES), f32), vmem((block, 2 * block), jnp.bfloat16),
            vmem((cells, lines), f32), vmem((cells, lines), f32),
            vmem((3, edge, lines), f32), vmem((3, edge, lines), f32),
            vmem((1, lines), f32), vmem((group, 1, lines), f32),
            vmem((2, 16, lines), f32), vmem((2, 16, lines), f32),
            vmem((8, LANES), f32), vmem((group, 8, LANES), f32),
            vmem((8, LANES), f32), vmem((bundles, 8, LANES), f32),
            dma((LOADS + 4,)), dma((group,)), dma((group,)), dma((2,)), dma((2,)),
            dma((group,)), dma((group,)), dma((bundles,)), dma((bundles,)),
        ],
        compiler_params=pltpu.CompilerParams(
            collective_id=0, has_side_effects=True, vmem_limit_bytes=48 * 2**20
        ),
        name="talk",
    )(
        fields, source, metric, jnp.asarray(const["weights"]),
    )


def join(coef, last, outer_l, inner_l, first, outer_r, inner_r):
    rp1, rp2, rm1, rm2, over, alpha, tau, kappa, scale = coef
    edge_l = rp2 * outer_r * over
    edge_r = rm2 * outer_l * over
    near_l = rp1 * outer_r + rp2 * inner_r - edge_l
    near_r = rm1 * outer_l + rm2 * inner_l - edge_r
    a = last + tau * near_l + edge_l
    b = first + tau * near_r + edge_r
    first_x = (b - kappa * a) * scale
    last_x = (a - kappa * b) * scale
    return near_l - alpha * first_x, edge_l, near_r - alpha * last_x, edge_r


def main_kernel(
    block, reach, rows_at_once,
    step_ref, fields_ref, register_ref, source_ref, metric_row_ref, curving_row_ref,
    offset_ref, halo_ref, maps_ref, columns_ref, joins_ref,
    new_fields_ref, new_register_ref, velocity_ref,
    inverse_ref, metric_ref, bent_ref, curving_ref, source_map_ref, field_map_ref,
    solved, carried, squeezed, firsts, lasts, cells_at, add,
):
    cells, lines = source_ref.shape
    parts = cells // block
    f32 = jnp.float32

    @pl.when(pl.program_id(0) == 0)
    def _():
        time_step = step_ref[0:1]
        fill_column(metric_ref, metric_row_ref, lambda values: time_step * values)
        fill_column(bent_ref, metric_row_ref, lambda values: time_step * values * values)
        fill_column(inverse_ref, metric_row_ref, lambda values: 1.0 / values)
        fill_column(curving_ref, curving_row_ref, lambda values: time_step * values)
        mask = lower_mask(block)
        source_map_ref[:block, :block] = mask
        source_map_ref[:block, block : 2 * block] = mask
        source_map_ref[:block, 2 * block :] = jnp.zeros((block, block), jnp.bfloat16)
        for m, (table, start) in enumerate(((source_map_ref, block), (field_map_ref, 0), (field_map_ref, block))):
            high, low = two_parts(maps_ref[m])
            table[start : start + block, :block] = high
            table[start : start + block, block : 2 * block] = high
            table[start : start + block, 2 * block :] = low

    def solve(k, c):
        rows = slice(k * block, (k + 1) * block)
        if c == 0:
            value = source_ref[rows] * spread(inverse_ref[rows], lines)
            table = source_map_ref
        else:
            value = fields_ref[c - 1, rows]
            table = field_map_ref
        high, low = two_parts(value)
        solved[k, c] = jnp.dot(table[...], jnp.concatenate([high, low, high], axis=0), preferred_element_type=f32)
        for s in systems[c]:
            start = places[s][1]
            firsts[c, k, s : s + 1] = solved[k, c, start : start + 1]
            lasts[c, k, s : s + 1] = solved[k, c, start + block - 1 : start + block]
            for e, r in enumerate((0, 1, block - 1, block - 2)):
                cells_at[c, k, e, s : s + 1] = value[r : r + 1]

    def far_cells(side, start):
        own = halo_ref[side, start : start + 4]
        return jnp.concatenate([own, own[1:4], jnp.zeros((1, lines), f32)], axis=0)

    def meet(c):
        def own(k, ends, outer, inner):
            return ends[c, k], cells_at[c, k, outer], cells_at[c, k, inner]

        _, _, near, at_edge = join(coef, halo_ref[0, 0:8], far_cells(0, 8), far_cells(0, 12), *own(0, firsts, 0, 1))
        add[c, 0, 0], add[c, 0, 1] = near * has_before, at_edge * has_before
        for k in range(parts - 1):
            add[c, k, 2], add[c, k, 3], add[c, k + 1, 0], add[c, k + 1, 1] = join(
                coef, *own(k, lasts, 2, 3), *own(k + 1, firsts, 0, 1)
            )
        k = parts - 1
        near, at_edge, _, _ = join(coef, *own(k, lasts, 2, 3), halo_ref[1, 0:8], far_cells(1, 8), far_cells(1, 12))
        add[c, k, 2], add[c, k, 3] = near * has_after, at_edge * has_after
        if c == 0:
            beyond = before[parts] * (1.0 - has_after)
            add[c, k, 2, 0:1] = add[c, k, 2, 0:1] + (NEAR_ONE + FAR_ONE - FAR_ONE / ALPHA_ONE) * beyond
            add[c, k, 3, 0:1] = add[c, k, 3, 0:1] + (FAR_ONE / ALPHA_ONE) * beyond
        for k in range(parts):
            for s in systems[c]:
                start = places[s][1]
                solved[k, c, start : start + 1] += add[c, k, 1, s : s + 1]
                solved[k, c, start + block - 1 : start + block] += add[c, k, 3, s : s + 1]

    def whole(k, c, s, r):
        start = places[s][1]
        kind = 0 if s < 4 else 1
        value = solved[k, c, start + r : start + r + rows_at_once]
        if r < reach[kind]:
            column = spread(columns_ref[2 * kind, r : r + rows_at_once], lines)
            value = value + column * add[c, k, 0, s : s + 1]
        if r + rows_at_once > block - reach[kind]:
            column = spread(columns_ref[2 * kind + 1, r : r + rows_at_once], lines)
            value = value + column * add[c, k, 2, s : s + 1]
        return value

    def finish(k, c):
        for r in range(0, block, rows_at_once):
            rows = slice(k * block + r, k * block + r + rows_at_once)
            if c == 0:
                stretch = spread(metric_ref[rows], lines)
                scaled = source_ref[rows] * spread(inverse_ref[rows], lines)
                velocity = 0.5 * scaled - (before[k] + solved[k, 0, r : r + rows_at_once])
                velocity_ref[rows] = velocity
                carried[rows] = velocity * stretch
                squeezed[rows] = stretch * whole(k, 0, 0, r)
            else:
                diffusion = DIFFUSIONS[c - 1]
                on_slope = spread(diffusion * curving_ref[rows], lines) - carried[rows]
                on_bend = spread(diffusion * bent_ref[rows], lines)
                field = fields_ref[c - 1, rows]
                change = on_slope * whole(k, c, c, r) + on_bend * whole(k, c, 3 + c, r) - field * squeezed[rows]
                updated = KEEP_FACTOR * register_ref[c - 1, rows] + change
                new_register_ref[c - 1, rows] = updated
                new_fields_ref[c - 1, rows] = field + STEP_FACTOR * updated

    places = [(0, block)] + [(1 + c, 0) for c in range(3)] + [(1 + c, block) for c in range(3)]
    systems = [[s for s in range(SYSTEMS) if places[s][0] == c] for c in range(4)]
    coef = [spread(joins_ref[i], lines) for i in range(9)]
    has_before, has_after = spread(step_ref[1:2], lines), spread(step_ref[2:3], lines)

    for k in range(parts):
        solve(k, 0)
    before = [offset_ref[0:1, :]]
    for k in range(parts):
        before.append(before[-1] + solved[k, 0, block - 1 : block])
    for c in range(1, 4):
        meet(c - 1)
        for k in range(parts):
            solve(k, c)
            finish(k, c - 1)
    meet(3)
    for k in range(parts):
        finish(k, 3)


def compute(fields, register, source, metric, curving, halo, offset, step, const, block):
    cells, lines = source.shape
    width = 256 if lines % 256 == 0 else LANES
    parts = cells // block
    f32 = jnp.float32

    def fixed(array):
        rank = array.ndim
        return pl.BlockSpec(array.shape, lambda j: (0,) * rank)

    three = pl.BlockSpec((3, cells, width), lambda j: (0, 0, j))
    flat = pl.BlockSpec((cells, width), lambda j: (0, j))
    maps, columns, joins = jnp.asarray(const["maps"]), jnp.asarray(const["columns"]), jnp.asarray(const["joins"])
    return pl.pallas_call(
        functools.partial(main_kernel, block, const["reach"], min(32, block)),
        grid=(lines // width,),
        out_shape=(
            jax.ShapeDtypeStruct(fields.shape, f32),
            jax.ShapeDtypeStruct(register.shape, f32),
            jax.ShapeDtypeStruct(source.shape, f32),
        ),
        in_specs=[
            fixed(step), three, three, flat, fixed(metric), fixed(curving),
            pl.BlockSpec((8, width), lambda j: (0, j)),
            pl.BlockSpec((2, 16, width), lambda j: (0, 0, j)),
            fixed(maps), fixed(columns), fixed(joins),
        ],
        out_specs=(three, three, flat),
        scratch_shapes=[
            *[pltpu.VMEM((cells, LANES), f32)] * 4,
            pltpu.VMEM((2 * block, 3 * block), jnp.bfloat16), pltpu.VMEM((2 * block, 3 * block), jnp.bfloat16),
            pltpu.VMEM((parts, 4, 2 * block, width), f32),
            pltpu.VMEM((cells, width), f32), pltpu.VMEM((cells, width), f32),
            pltpu.VMEM((4, parts, 8, width), f32), pltpu.VMEM((4, parts, 8, width), f32),
            pltpu.VMEM((4, parts, 4, 8, width), f32), pltpu.VMEM((4, parts, 4, 8, width), f32),
        ],
        compiler_params=pltpu.CompilerParams(vmem_limit_bytes=48 * 2**20),
        name="compute",
    )(
        step, fields, register, source, metric, curving, offset, halo, maps, columns, joins,
    )


def local(fields, register, source, metric, curvature):
    group, bundles = lax.axis_size("gx"), lax.axis_size("gz")
    cells = source.shape[0]
    block = min(256, cells)
    const = tables(block)
    metric_row, curving_row = metric.reshape(1, cells), curvature.reshape(1, cells)
    halo, offset, step = talk(fields, source, metric_row, const, group, bundles, block)
    return compute(fields, register, source, metric_row, curving_row, halo, offset, step, const, block)


def solution(mesh):
    placed = (P(None, "gx", "gz"), P(None, "gx", "gz"), P("gx", "gz"), P("gx"), P("gx"))
    return jax.shard_map(
        local,
        mesh=mesh,
        in_specs=placed,
        out_specs=(P(None, "gx", "gz"), P(None, "gx", "gz"), P("gx", "gz")),
        check_vma=False,
    )
```
